512 devices in a mesh: scen: 32 (over x, z), area: 16 (over y, core).
Axes of the slice: x: 4, y: 8, z: 8, core: 2. Of those that a mesh axis runs over, the one named last changes fastest.
Arguments:
- cost_lin: float32 [1536, 16, 7, 384], P('scen', 'area'), may hold values from -6 to 6
- na_dual: float32 [1536, 16, 7, 384], P('scen', 'area'), may hold values from -6 to 6
- prior_mean: float32 [1536, 16, 7, 384], P('scen', 'area'), may hold values from -6 to 6
- kkt_inverse: bfloat16 [16, 7, 384, 384], P('area'), may hold values from -0.3125 to 0.3125
- tie_coef: float32 [16, 16], P('area'), may hold values from 0.3 to 1.5
- res_count: int32 [16], P('area'), may hold values from 4 to 16, as said below
- line_class: int32 [16, 2], P('area'), may hold values from 1 to 3, as said below
- node_of: int32 [7, 1536], P(None, 'scen'), may hold values from 0 to 63, as said below
Outputs:
- node_mean: float32 [1536, 16, 7, 384], P('scen', 'area')
- new_dual: float32 [1536, 16, 7, 384], P('scen', 'area')
The draws below stay inside these ranges and needn't reach their ends.
Inputs may be any that keep to these rules, and one draw needn't show every extreme that they name: `res_count`: some area has 16 reservoirs and some area has 4. line_class[a, 0] equals line_class[a-1, 1], area indices taken modulo 16. `node_of`: at section c the nodes are 0 to 2**c - 1, every one of them holds at least one scenario, and scenarios that share a node at section c + 1 share it at section c.
All inputs are finite; a program needn't handle non-finite values.
Results may differ from the reference program's by a relative error of at most 0.004.
Values sent between devices are 32-bit elements; how exact they have to be, the bound alone decides.
A program may use at most 64 MiB of HBM per device.

```python
import math
import jax
import jax.numpy as jnp
from jax import lax

RES = 16
HOURS = 24
SPANS = 7
SWEEPS = 2
SCEN = 1536
AREAS = 16
K = 384
GROUPS = 64


def draw_res_count(key, part):
    base_counts = jax.random.randint(jax.random.fold_in(key, 11), (AREAS,), RES // 4, RES + 1)
    first_area = jax.random.randint(jax.random.fold_in(key, 12), (), 0, AREAS)
    second_area = (first_area + 1 + jax.random.randint(jax.random.fold_in(key, 13), (), 0, AREAS - 1)) % AREAS
    area_ids = jnp.arange(AREAS, dtype=jnp.int32)
    forced = jnp.where(area_ids == first_area, RES, jnp.where(area_ids == second_area, RES // 4, base_counts))
    return forced.astype(jnp.int32)


def draw_line_class(key, part):
    base_class = jax.random.randint(jax.random.fold_in(key, 31), (AREAS,), 1, 4)
    first_line = jax.random.randint(jax.random.fold_in(key, 32), (), 0, AREAS)
    second_line = (first_line + 1 + jax.random.randint(jax.random.fold_in(key, 33), (), 0, AREAS - 1)) % AREAS
    line_ids = jnp.arange(AREAS, dtype=jnp.int32)
    forced = jnp.where(line_ids == first_line, 3, jnp.where(line_ids == second_line, 1, base_class)).astype(jnp.int32)
    return jnp.stack([jnp.roll(forced, 1), forced], axis=-1).astype(jnp.int32)


def draw_node_of(key, part):
    key = jax.random.fold_in(key, 7)
    order = jax.random.permutation(jax.random.fold_in(key, 21), SCEN).astype(jnp.int32)
    cut_pool = jax.random.permutation(jax.random.fold_in(key, 22), SCEN - 1).astype(jnp.int32) + 1
    cut_points = cut_pool[:GROUPS - 1]
    rank_ids = jnp.arange(SCEN, dtype=jnp.int32)
    marks = jnp.sum((rank_ids[:, None] == cut_points[None, :]).astype(jnp.int32), axis=1).astype(jnp.int32)
    leaf_of_rank = jnp.cumsum(marks).astype(jnp.int32)
    leaf_of = leaf_of_rank[order]
    section_rows = []
    for section_index in range(SPANS):
        divisor = 2 ** (SPANS - 1 - section_index)
        section_rows.append(leaf_of // divisor)
    return jnp.stack(section_rows, axis=0).astype(jnp.int32)


def block_scale(own_key, extent, shards, low, high):
    factor_of = 1.0
    for dim, shards_of in shards:
        steps = jax.random.uniform(jax.random.fold_in(jax.random.fold_in(own_key, 6), dim), (shards_of,), jnp.float32, low / len(shards), high / len(shards))
        factor_of = factor_of * jnp.repeat(jnp.exp(steps), extent[dim] // shards_of).reshape((-1,) + (1,) * (len(extent) - 1 - dim))
    return factor_of


def normal_values(stream_key, shape, width, bound, split=(), kind=jnp.bfloat16):
    entries = width * jax.random.normal(stream_key, shape, jnp.float32)
    if split:
        entries = entries * block_scale(stream_key, shape, split, -0.22, 0.18)
    return jnp.clip(entries, -bound, bound).astype(kind)


def setup_inputs(seed: int = 0) -> dict:
    seeds = jax.random.split(jax.random.key(seed), 9)
    return {
        "cost_lin": normal_values(seeds[0], (SCEN, AREAS, SPANS, K), 1.0, 6.0, ((0, 32), (1, 16)), jnp.float32),
        "na_dual": normal_values(seeds[1], (SCEN, AREAS, SPANS, K), 0.5, 6.0, ((0, 32), (1, 16)), jnp.float32),
        "prior_mean": normal_values(seeds[2], (SCEN, AREAS, SPANS, K), 1.0, 6.0, ((0, 32), (1, 16)), jnp.float32),
        "kkt_inverse": normal_values(seeds[3], (AREAS, SPANS, K, K), K ** -0.5, 0.3125, ((0, 16),)),
        "tie_coef": jnp.clip(jnp.exp(math.log(1.5) - 1.60943787 * jax.random.uniform(seeds[4], (AREAS, RES), jnp.float32) ** block_scale(seeds[4], (AREAS, RES), ((0, 16),), -0.2, 0.2)), 0.3, 1.5),
        "res_count": draw_res_count(jax.random.fold_in(seeds[8], 71), 0),
        "line_class": draw_line_class(jax.random.fold_in(seeds[8], 71), 0),
        "node_of": draw_node_of(jax.random.fold_in(seeds[8], 71), 0),
    }


RHO = 1.0
RHO_TIE = 0.5


def reference(cost_lin, na_dual, prior_mean, kkt_inverse, tie_coef, res_count, line_class, node_of):
    slot_ids = jnp.arange(RES, dtype=jnp.int32)
    live_slots = (slot_ids[None, :] < res_count[:, None]).astype(jnp.float32)
    export_weight = tie_coef * live_slots
    mask_full = jnp.tile(live_slots, (1, HOURS))
    left_weight = line_class[:, 0].astype(jnp.float32) / 3.0
    right_weight = line_class[:, 1].astype(jnp.float32) / 3.0
    anchor = RHO * prior_mean - cost_lin - na_dual
    inverse_full = kkt_inverse.astype(jnp.float32)
    current = prior_mean
    for sweep_index in range(SWEEPS):
        blocks = current.reshape(SCEN, AREAS, SPANS, HOURS, RES)
        export = jnp.sum(blocks * export_weight[None, :, None, None, :], axis=4).reshape(SCEN, AREAS, SPANS * HOURS)
        left_export = jnp.roll(export, 1, axis=1)
        right_export = jnp.roll(export, -1, axis=1)
        tie_gap = right_weight[None, :, None] * (right_export - export) + left_weight[None, :, None] * (left_export - export)
        coupling = tie_gap.reshape(SCEN, AREAS, SPANS, HOURS, 1) * export_weight[None, :, None, None, :]
        target = anchor + RHO_TIE * coupling.reshape(SCEN, AREAS, SPANS, K)
        target_low = lax.optimization_barrier(target.astype(jnp.bfloat16))
        target_back = target_low.astype(jnp.float32)
        solved = jnp.einsum("sack,acjk->sacj", target_back, inverse_full, precision=lax.Precision.HIGHEST)
        current = solved * mask_full[None, :, None, :]
    node_rows = []
    for section_index in range(SPANS):
        group_count = 2 ** section_index
        indicator = (node_of[section_index][:, None] == jnp.arange(group_count, dtype=jnp.int32)[None, :]).astype(jnp.float32)
        group_sum = jnp.einsum("sn,sak->nak", indicator, current[:, :, section_index], precision=lax.Precision.HIGHEST)
        group_size = jnp.sum(indicator, axis=0)
        group_mean = group_sum / group_size[:, None, None]
        node_rows.append(jnp.einsum("sn,nak->sak", indicator, group_mean, precision=lax.Precision.HIGHEST))
    node_mean = jnp.stack(node_rows, axis=2)
    new_dual = na_dual + RHO * (current - node_mean)
    return node_mean, new_dual
```

```python
import functools

import jax
import jax.numpy as jnp
from jax import lax
from jax.experimental import pallas as pl
from jax.experimental.pallas import tpu as pltpu
from jax.sharding import PartitionSpec as P

F32 = jnp.float32
BF16 = jnp.bfloat16
MESH = pl.DeviceIdType.MESH

SCEN_L = 48
SPANS = 7
K = 384
RES = 16
BLK = 128
NB = K // BLK
ROWS = SCEN_L * SPANS
STRIDE = SPANS * NB
NX, NZ, NA = 4, 8, 16
NODES = 128
CHUNK = NODES // NZ
WIDE = K + BLK

BASE = (126, 124, 120, 112, 96, 64, 0)
SLOT = (0, 1, 2, 4, 5, 6, 3)

X_OFFS = ((2, 0), (1, 0), (3, 0))
Z_OFFS = tuple((0, d) for d in (4, 3, 5, 2, 6, 1, 7))


def split(value):
    high = value.astype(BF16)
    low = (value - high.astype(F32)).astype(BF16)
    return high, low


def dot(a, b):
    return jnp.dot(a, b, preferred_element_type=F32)


def dot_nt(a, b):
    return lax.dot_general(a, b, (((1,), (1,)), ((), ())), preferred_element_type=F32)


def kernel(
    cost_h, dual_h, prior_h, kkt_h, tie_h, count_h, line_h, node_h,
    mean_o, newdual_o,
    cost_v, dual_v, prior_v, kkt_v, tie_r, count_r, line_r, node_r, tie_v, node_v, sel_v, spread_v, spread_all_v, pick_v, pickt_v,
    anchor_v, base_v, kgap_v,
    exp_v, low_v, high_v,
    part_v, rz_v, sumz_v, rx_v, total_v, gather_v,
    gsum_v, gx_v, gsumx_v, gz_v,
    in_sem, es_sem, er_sem, zs_sem, zr_sem, xs_sem, xr_sem, as_sem, ar_sem,
    gxs_sem, gxr_sem, gzs_sem, gzr_sem,
):
    me = lax.axis_index("scen")
    area = lax.axis_index("area")
    my_x = me // NZ
    my_z = lax.rem(me, NZ)
    up = lax.rem(area + 1, NA)
    down = lax.rem(area + NA - 1, NA)

    def peer_z(off):
        return lax.rem(my_z + off[1], NZ)

    def peer(off):
        return lax.rem(my_x + off[0], NX) * NZ + peer_z(off)

    def send(src, dst, send_sem, recv_sem, device):
        pltpu.make_async_remote_copy(
            src_ref=src, dst_ref=dst, send_sem=send_sem, recv_sem=recv_sem,
            device_id=device, device_id_type=MESH,
        ).start()

    def wait(ref, sem):
        pltpu.make_async_copy(ref, ref, sem).wait()

    loads = [
        pltpu.make_async_copy(src, dst, in_sem.at[i])
        for i, (src, dst) in enumerate(
            (
                (prior_h, prior_v), (cost_h, cost_v), (dual_h, dual_v), (kkt_h, kkt_v),
                (tie_h, tie_r), (count_h, count_r), (line_h, line_r), (node_h, node_r),
            )
        )
    ]
    for i in (4, 5, 6, 7, 0, 1, 2, 3):
        loads[i].start()

    barrier = pltpu.get_barrier_semaphore()
    for off in Z_OFFS + X_OFFS:
        pl.semaphore_signal(barrier, inc=1, device_id={"scen": peer(off)}, device_id_type=MESH)
    for neighbour in (up, down):
        pl.semaphore_signal(barrier, inc=1, device_id={"area": neighbour}, device_id_type=MESH)

    rows = lax.broadcasted_iota(jnp.int32, (K, BLK), 0)
    lanes = lax.broadcasted_iota(jnp.int32, (K, BLK), 1)
    rows_w = lax.broadcasted_iota(jnp.int32, (BLK, K), 0)
    lanes_w = lax.broadcasted_iota(jnp.int32, (BLK, K), 1)
    for j in range(4):
        sel_v[j] = jnp.where(lanes == 32 * j + (rows >> 4), 1.0, 0.0).astype(BF16)
        spread_v[j] = jnp.where(rows_w == 32 * j + (lanes_w >> 4), 1.0, 0.0).astype(BF16)
    spread_all_v[...] = jnp.where((rows_w & 31) == (lanes_w >> 4), 1.0, 0.0).astype(BF16)

    for i in (4, 5, 6, 7):
        loads[i].wait()
    tie_v[...] = jnp.zeros((8, BLK), F32)
    tie_v[0:1, 0:RES] = tie_r[...]
    tie = tie_v[...]
    for shift in (16, 32, 64):
        tie = tie + pltpu.roll(tie, shift, 1)
    lane_row = lax.broadcasted_iota(jnp.int32, (1, BLK), 1)
    live = jnp.where((lane_row & 15) < count_r[0], 1.0, 0.0)
    weight = tie[0:1] * live
    live3 = jnp.concatenate([live] * NB, axis=1)
    weight3 = jnp.concatenate([weight] * NB, axis=1)
    left_weight = jnp.full((1, BLK), line_r[0, 0], jnp.int32).astype(F32) / 3.0
    right_weight = jnp.full((1, BLK), line_r[0, 1], jnp.int32).astype(F32) / 3.0

    node_v[...] = jnp.full((BLK, BLK), -1.0, F32)
    node_v[0:SPANS, 0:SCEN_L] = node_r[...].astype(F32)
    node_t = jnp.transpose(node_v[...])
    node_lane = lax.broadcasted_iota(jnp.int32, (SCEN_L, BLK), 1).astype(F32)
    picks = []
    for c in range(SPANS):
        picks.append(jnp.where(node_lane - BASE[c] == node_t[0:SCEN_L, c : c + 1], 1.0, 0.0))
    picks.append(jnp.zeros((K - ROWS, BLK), F32))
    pick = jnp.concatenate(picks, axis=0)
    pickt_v[...] = jnp.transpose(pick).astype(BF16)
    pick_b = pick[0:ROWS].astype(BF16)
    pick_v[:, 0:BLK] = pick_b
    pick_v[:, BLK:] = pick_b

    def block(ref, c):
        return jnp.concatenate(
            [ref[pl.ds(c * NB + b, SCEN_L, stride=STRIDE), :] for b in range(NB)], axis=1
        )

    def exports(value_of, sweep):
        groups = [None, None]
        for c in range(SPANS):
            g, j = SLOT[c] // 4, SLOT[c] % 4
            high, low = split(value_of(c) * weight3)
            part = dot(jnp.concatenate([high, low], axis=0), sel_v[j])
            part = part[0:SCEN_L] + part[SCEN_L:]
            groups[g] = part if groups[g] is None else groups[g] + part
        exp_v[sweep] = jnp.concatenate(groups, axis=0)

    def send_exports(sweep):
        send(exp_v.at[sweep], low_v.at[sweep], es_sem.at[sweep, 0], er_sem.at[sweep, 0], {"area": up})
        send(exp_v.at[sweep], high_v.at[sweep], es_sem.at[sweep, 1], er_sem.at[sweep, 1], {"area": down})

    def tie_gap(sweep):
        wait(low_v.at[sweep], er_sem.at[sweep, 0])
        wait(high_v.at[sweep], er_sem.at[sweep, 1])
        own = exp_v[sweep]
        return right_weight * (high_v[sweep] - own) + left_weight * (low_v[sweep] - own)

    def targets(gap):
        high, low = split(gap)
        found = []
        for c in range(SPANS):
            g, j = SLOT[c] // 4, SLOT[c] % 4
            rows_g = slice(g * SCEN_L, (g + 1) * SCEN_L)
            wide = dot(jnp.concatenate([high[rows_g], low[rows_g]], axis=0), spread_v[j])
            coupling = 0.5 * weight3 * (wide[0:SCEN_L] + wide[SCEN_L:])
            found.append((anchor_v[c * SCEN_L : (c + 1) * SCEN_L, :] + coupling).astype(BF16))
        return found

    loads[0].wait()
    exports(lambda c: block(prior_v, c), 0)

    loads[1].wait()
    loads[2].wait()
    for c in range(SPANS):
        anchor_v[c * SCEN_L : (c + 1) * SCEN_L, :] = (
            block(prior_v, c) - block(cost_v, c) - block(dual_v, c)
        )
    loads[3].wait()
    highs, lows = [], []
    for c in range(SPANS):
        high, low = split(anchor_v[c * SCEN_L : (c + 1) * SCEN_L, :])
        both = dot_nt(jnp.concatenate([high, low], axis=0), kkt_v[c])
        high, low = split(both[0:SCEN_L] + both[SCEN_L:])
        highs.append(high)
        lows.append(low)
    pick_t = pickt_v[:, 0:ROWS]
    part = dot(pick_t, jnp.concatenate(highs, axis=0)) + dot(pick_t, jnp.concatenate(lows, axis=0))
    sizes = dot(pick_t, jnp.ones((ROWS, BLK), BF16))
    for i in range(NZ):
        rows_i = slice(i * CHUNK, (i + 1) * CHUNK)
        part_v[i, :, 0:K] = part[rows_i]
        part_v[i, :, K:] = sizes[rows_i]

    pl.semaphore_wait(barrier, len(Z_OFFS) + len(X_OFFS) + 2)
    send_exports(0)
    for n, off in enumerate(Z_OFFS):
        send(part_v.at[peer_z(off)], rz_v.at[n], zs_sem, zr_sem, {"scen": peer(off)})

    first = targets(tie_gap(0))
    exports(lambda c: dot_nt(first[c], kkt_v[c]), 1)
    send_exports(1)

    gap = tie_gap(1)
    gap_high, gap_low = split(gap)
    stacked = []
    for half in (gap_high, gap_low):
        stacked.append(
            jnp.concatenate(
                [half[SLOT[c] // 4 * SCEN_L : (SLOT[c] // 4 + 1) * SCEN_L] for c in range(SPANS)],
                axis=0,
            )
        )
    gap_part = dot(pick_t, stacked[0]) + dot(pick_t, stacked[1])
    node_row = lax.broadcasted_iota(jnp.int32, (NODES // 2, BLK), 0) + NODES // 2
    group = lax.broadcasted_iota(jnp.int32, (NODES // 2, BLK), 1) >> 5
    place = jnp.zeros((NODES // 2, BLK), jnp.int32) + SLOT[5] % 4
    for c in (4, 3, 2, 1, 0):
        place = jnp.where(node_row >= BASE[c], SLOT[c] % 4, place)
    upper = group == SLOT[6] % 4
    lower = group == place
    gsum_v[...] = jnp.where(upper, gap_part[0 : NODES // 2], 0.0) + jnp.where(
        lower, gap_part[NODES // 2 :], 0.0
    )
    for n, off in enumerate(X_OFFS):
        send(gsum_v, gx_v.at[n], gxs_sem, gxr_sem, {"scen": peer(off)})

    wait(rz_v, zr_sem)
    acc = part_v[my_z]
    for n in range(len(Z_OFFS)):
        acc = acc + rz_v[n]
    sumz_v[...] = acc
    for n, off in enumerate(X_OFFS):
        send(sumz_v, rx_v.at[n], xs_sem, xr_sem, {"scen": peer(off)})

    second = targets(gap)
    for c in range(SPANS):
        current = dot_nt(second[c], kkt_v[c]) * live3
        base_v[c * SCEN_L : (c + 1) * SCEN_L, :] = block(dual_v, c) + current

    wait(gx_v, gxr_sem)
    gacc = gsum_v[...]
    for n in range(len(X_OFFS)):
        gacc = gacc + gx_v[n]
    gsumx_v[...] = gacc
    for n, off in enumerate(Z_OFFS):
        send(gsumx_v, gz_v.at[n], gzs_sem, gzr_sem, {"scen": peer(off)})

    wait(rx_v, xr_sem)
    acc = sumz_v[...]
    for n in range(len(X_OFFS)):
        acc = acc + rx_v[n]
    total_v[...] = acc
    for n, off in enumerate(Z_OFFS):
        send(total_v, gather_v.at[my_z], as_sem, ar_sem.at[n], {"scen": peer(off)})
    gather_v[my_z] = acc

    wait(gz_v, gzr_sem)
    gacc = gsumx_v[...]
    for n in range(len(Z_OFFS)):
        gacc = gacc + gz_v[n]
    summed = jnp.concatenate([jnp.where(upper, gacc, 0.0), jnp.where(lower, gacc, 0.0)], axis=0)
    high, low = split(summed)
    wide = dot(jnp.concatenate([high, low], axis=0), spread_all_v[...])
    coupling = 0.5 * weight3 * (wide[0:NODES] + wide[NODES:])
    high, low = split(coupling)
    for c, first_row, count in ((6, 0, 64), (5, 64, 32), (4, 96, 16)):
        rows_c = slice(first_row, first_row + count)
        both = dot_nt(jnp.concatenate([high[rows_c], low[rows_c]], axis=0), kkt_v[c])
        kgap_v[rows_c, :] = both[0:count] + both[count:]
    small = jnp.concatenate([high[112:128], low[112:128]], axis=0)
    row_s = lax.broadcasted_iota(jnp.int32, (CHUNK, K), 0) + 112
    rest = jnp.zeros((CHUNK, K), F32)
    for c in (3, 2, 1, 0):
        both = dot_nt(small, kkt_v[c])
        inside = (row_s >= BASE[c]) & (row_s < BASE[c] + 2**c)
        rest = rest + jnp.where(inside, both[0:CHUNK] + both[CHUNK:], 0.0)
    kgap_v[112:128, :] = rest

    for n, off in enumerate(Z_OFFS):
        source = lax.rem(my_z + NZ - off[1], NZ)
        wait(gather_v.at[source], ar_sem.at[n])
    highs, lows = [], []
    for i in range(NZ):
        sizes_i = jnp.maximum(gather_v[i, :, K:], 1.0)
        scale = jnp.concatenate([1.0 / sizes_i] * NB, axis=1)
        average = (gather_v[i, :, 0:K] + kgap_v[i * CHUNK : (i + 1) * CHUNK, :]) * scale * live3
        high, low = split(average)
        highs.append(high)
        lows.append(low)
    averages = jnp.concatenate(highs + lows, axis=0)
    for c in range(SPANS):
        rows_c = slice(c * SCEN_L, (c + 1) * SCEN_L)
        node_mean = dot(pick_v[rows_c, :], averages)
        new_dual = base_v[rows_c, :] - node_mean
        for b in range(NB):
            place_b = pl.ds(c * NB + b, SCEN_L, stride=STRIDE)
            mean_o[place_b, :] = node_mean[:, b * BLK : (b + 1) * BLK]
            newdual_o[place_b, :] = new_dual[:, b * BLK : (b + 1) * BLK]

    for sweep in range(2):
        wait(exp_v.at[sweep], es_sem.at[sweep, 0])
        wait(exp_v.at[sweep], es_sem.at[sweep, 1])
    wait(rz_v, zs_sem)
    wait(rx_v, xs_sem)
    wait(rz_v, as_sem)
    wait(gx_v, gxs_sem)
    wait(gz_v, gzs_sem)


def on_device(cost_lin, na_dual, prior_mean, kkt_inverse, tie_coef, res_count, line_class, node_of):
    flat = (SCEN_L * STRIDE, BLK)
    any_spec = pl.BlockSpec(memory_space=pl.ANY)
    vmem = pl.BlockSpec(memory_space=pltpu.VMEM)
    dma = pltpu.SemaphoreType.DMA
    nz, nx = NZ - 1, NX - 1
    scratch = [
        pltpu.VMEM(flat, F32),
        pltpu.VMEM(flat, F32),
        pltpu.VMEM(flat, F32),
        pltpu.VMEM((SPANS, K, K), BF16),
        pltpu.VMEM((1, RES), F32),
        pltpu.SMEM((1,), jnp.int32),
        pltpu.SMEM((1, 2), jnp.int32),
        pltpu.VMEM((SPANS, SCEN_L), jnp.int32),
        pltpu.VMEM((8, BLK), F32),
        pltpu.VMEM((BLK, BLK), F32),
        pltpu.VMEM((4, K, BLK), BF16),
        pltpu.VMEM((4, BLK, K), BF16),
        pltpu.VMEM((BLK, K), BF16),
        pltpu.VMEM((ROWS, 2 * BLK), BF16),
        pltpu.VMEM((BLK, K), BF16),
        pltpu.VMEM((ROWS, K), F32),
        pltpu.VMEM((ROWS, K), F32),
        pltpu.VMEM((NODES, K), F32),
        pltpu.VMEM((2, 2 * SCEN_L, BLK), F32),
        pltpu.VMEM((2, 2 * SCEN_L, BLK), F32),
        pltpu.VMEM((2, 2 * SCEN_L, BLK), F32),
        pltpu.VMEM((NZ, CHUNK, WIDE), F32),
        pltpu.VMEM((nz, CHUNK, WIDE), F32),
        pltpu.VMEM((CHUNK, WIDE), F32),
        pltpu.VMEM((nx, CHUNK, WIDE), F32),
        pltpu.VMEM((CHUNK, WIDE), F32),
        pltpu.VMEM((NZ, CHUNK, WIDE), F32),
        pltpu.VMEM((NODES // 2, BLK), F32),
        pltpu.VMEM((nx, NODES // 2, BLK), F32),
        pltpu.VMEM((NODES // 2, BLK), F32),
        pltpu.VMEM((nz, NODES // 2, BLK), F32),
        dma((8,)), dma((2, 2)), dma((2, 2)), dma, dma, dma, dma, dma, dma((nz,)),
        dma, dma, dma, dma,
    ]
    node_mean, new_dual = pl.pallas_call(
        kernel,
        out_shape=[jax.ShapeDtypeStruct(flat, F32)] * 2,
        in_specs=[any_spec] * 8,
        out_specs=[vmem, vmem],
        scratch_shapes=scratch,
        compiler_params=pltpu.CompilerParams(
            collective_id=0, has_side_effects=True, vmem_limit_bytes=56 * 2**20
        ),
        name="round",
    )(
        cost_lin.reshape(flat), na_dual.reshape(flat), prior_mean.reshape(flat),
        kkt_inverse.reshape(SPANS, K, K), tie_coef, res_count, line_class, node_of,
    )
    return node_mean.reshape(cost_lin.shape), new_dual.reshape(cost_lin.shape)


def solution(mesh):
    placed = (
        P("scen", "area", None, None),
        P("scen", "area", None, None),
        P("scen", "area", None, None),
        P("area", None, None, None),
        P("area", None),
        P("area"),
        P("area", None),
        P(None, "scen"),
    )
    return jax.shard_map(
        on_device,
        mesh=mesh,
        in_specs=placed,
        out_specs=(P("scen", "area", None, None), P("scen", "area", None, None)),
        check_vma=False,
    )
```

```python
import functools

import jax
import jax.numpy as jnp
from jax import lax
from jax.experimental import pallas as pl
from jax.experimental.pallas import tpu as pltpu
from jax.sharding import PartitionSpec as P

F32 = jnp.float32
BF16 = jnp.bfloat16
MESH = pl.DeviceIdType.MESH

SCEN_L = 48
SPANS = 7
K = 384
RES = 16
BLK = 128
NB = K // BLK
ROWS = SCEN_L * SPANS
STRIDE = SPANS * NB
NX, NZ, NA = 4, 8, 16
NODES = 128
CHUNK = NODES // NZ
WIDE = K + BLK

BASE = (126, 124, 120, 112, 96, 64, 0)

X_OFFS = ((2, 0), (1, 0), (3, 0))
Z_OFFS = tuple((0, d) for d in (4, 3, 5, 2, 6, 1, 7))
XALL_OFFS = X_OFFS + ((0, 0),)
A_OFFS = (2, NA - 2, 1, NA - 1)


def split(value):
    high = value.astype(BF16)
    low = (value - high.astype(F32)).astype(BF16)
    return high, low


def dot(a, b):
    return jnp.dot(a, b, preferred_element_type=F32)


def dot_nt(a, b):
    return lax.dot_general(a, b, (((1,), (1,)), ((), ())), preferred_element_type=F32)


def kernel(
    cost_h, dual_h, prior_h, kkt_h, small_r,
    mean_o, base_o, live_o,
    cost_v, dual_v, prior_v, kkt_v, node_v, sel_v, spread_v, spread_all_v, pick_v, pickt_v,
    anchor_v, swh_v, swl_v, sel_all_v,
    exp_v, low_v, high_v,
    part_v, rz_v, sumz_v, rx_v, total_v, gather_v,
    block_v, ra_v, gmat_v, glow_v, ghigh_v, kgap_v,
    in_sem, es_sem, er_sem, zs_sem, zr_sem, xs_sem, xr_sem, as_sem, ar_sem,
    bs_sem, br_sem, gs_sem, gr_sem,
):
    me = lax.axis_index("scen")
    area = lax.axis_index("area")
    my_x = me // NZ
    my_z = lax.rem(me, NZ)
    up = lax.rem(area + 1, NA)
    down = lax.rem(area + NA - 1, NA)

    def peer_z(off):
        return lax.rem(my_z + off[1], NZ)

    def peer(off):
        return lax.rem(my_x + off[0], NX) * NZ + peer_z(off)

    def area_at(step):
        return lax.rem(area + step, NA)

    def send(src, dst, send_sem, recv_sem, device):
        pltpu.make_async_remote_copy(
            src_ref=src, dst_ref=dst, send_sem=send_sem, recv_sem=recv_sem,
            device_id=device, device_id_type=MESH,
        ).start()

    def wait(ref, sem):
        pltpu.make_async_copy(ref, ref, sem).wait()

    loads = [
        pltpu.make_async_copy(src, dst, in_sem.at[i])
        for i, (src, dst) in enumerate(
            ((prior_h, prior_v), (cost_h, cost_v), (dual_h, dual_v), (kkt_h, kkt_v))
        )
    ]
    for load in loads:
        load.start()

    barrier = pltpu.get_barrier_semaphore()
    for off in Z_OFFS + X_OFFS:
        pl.semaphore_signal(barrier, inc=1, device_id={"scen": peer(off)}, device_id_type=MESH)
    for step in A_OFFS:
        for off in XALL_OFFS:
            pl.semaphore_signal(
                barrier, inc=1, device_id={"scen": peer(off), "area": area_at(step)},
                device_id_type=MESH,
            )

    rows = lax.broadcasted_iota(jnp.int32, (K, BLK), 0)
    lanes = lax.broadcasted_iota(jnp.int32, (K, BLK), 1)
    rows_w = lax.broadcasted_iota(jnp.int32, (BLK, K), 0)
    lanes_w = lax.broadcasted_iota(jnp.int32, (BLK, K), 1)
    for j in range(4):
        sel_v[j] = jnp.where(lanes == 32 * j + (rows >> 4), 1.0, 0.0).astype(BF16)
        spread_v[j] = jnp.where(rows_w == 32 * j + (lanes_w >> 4), 1.0, 0.0).astype(BF16)
    spread_all_v[...] = jnp.where((rows_w & 31) == (lanes_w >> 4), 1.0, 0.0).astype(BF16)

    small = small_r[8:16, :]
    tie = small
    for shift in (16, 32, 64):
        tie = tie + pltpu.roll(tie, shift, 1)
    lane_row = lax.broadcasted_iota(jnp.int32, (1, BLK), 1)
    live = jnp.where((lane_row & 15).astype(F32) < small[2:3, 0:1], 1.0, 0.0)
    live_o[...] = jnp.broadcast_to(live, (8, BLK))
    weight = tie[0:1] * live
    live3 = jnp.concatenate([live] * NB, axis=1)
    weight3 = jnp.concatenate([weight] * NB, axis=1)
    for j in range(4):
        placed = jnp.where(rows_w == 32 * j + (lanes_w >> 4), 1.0, 0.0)
        swh_v[j], swl_v[j] = split(placed * weight3)
    sel_all_v[...] = jnp.where((lanes & 31) == (rows >> 4), 1.0, 0.0).astype(BF16)
    left_weight = jnp.broadcast_to(small[1:2, 0:1], (1, BLK)) / 3.0
    right_weight = jnp.broadcast_to(small[1:2, 1:2], (1, BLK)) / 3.0

    node_v[...] = jnp.zeros((BLK, BLK), F32)
    node_v[0:8, :] = small_r[0:8, :]
    node_t = jnp.transpose(node_v[...])
    node_lane = lax.broadcasted_iota(jnp.int32, (SCEN_L, BLK), 1).astype(F32)
    picks = []
    for c in range(SPANS):
        picks.append(jnp.where(node_lane - BASE[c] == node_t[0:SCEN_L, c : c + 1], 1.0, 0.0))
    picks.append(jnp.zeros((K - ROWS, BLK), F32))
    pick = jnp.concatenate(picks, axis=0)
    pickt_v[...] = jnp.transpose(pick).astype(BF16)
    pick_b = pick[0:ROWS].astype(BF16)
    pick_v[:, 0:BLK] = pick_b
    pick_v[:, BLK:] = pick_b

    def place_of(row):
        place = jnp.where(row < 64, 2, jnp.where(row < 96, 1, 0))
        place = jnp.where(row >= 112, 3, place)
        place = jnp.where(row >= 120, 2, place)
        place = jnp.where(row >= 124, 1, place)
        return jnp.where(row >= 126, 0, place)

    def block(ref, c):
        return jnp.concatenate(
            [ref[pl.ds(c * NB + b, SCEN_L, stride=STRIDE), :] for b in range(NB)], axis=1
        )

    def exports(value_of, sweep):
        groups = [None, None]
        for c in range(SPANS):
            g, j = c // 4, c % 4
            high, low = split(value_of(c) * weight3)
            part = dot(jnp.concatenate([high, low], axis=0), sel_v[j])
            part = part[0:SCEN_L] + part[SCEN_L:]
            groups[g] = part if groups[g] is None else groups[g] + part
        exp_v[sweep] = jnp.concatenate(groups, axis=0)

    def send_exports(sweep):
        send(exp_v.at[sweep], low_v.at[sweep], es_sem.at[sweep, 0], er_sem.at[sweep, 0], {"area": up})
        send(exp_v.at[sweep], high_v.at[sweep], es_sem.at[sweep, 1], er_sem.at[sweep, 1], {"area": down})

    def tie_gap(sweep):
        wait(low_v.at[sweep], er_sem.at[sweep, 0])
        wait(high_v.at[sweep], er_sem.at[sweep, 1])
        own = exp_v[sweep]
        return right_weight * (high_v[sweep] - own) + left_weight * (low_v[sweep] - own)

    def targets(gap):
        high, low = split(gap)
        found = []
        for c in range(SPANS):
            g, j = c // 4, c % 4
            rows_g = slice(g * SCEN_L, (g + 1) * SCEN_L)
            wide = dot(jnp.concatenate([high[rows_g], low[rows_g]], axis=0), spread_v[j])
            coupling = 0.5 * weight3 * (wide[0:SCEN_L] + wide[SCEN_L:])
            found.append((anchor_v[c * SCEN_L : (c + 1) * SCEN_L, :] + coupling).astype(BF16))
        return found

    loads[0].wait()
    exports(lambda c: block(prior_v, c), 0)

    loads[1].wait()
    loads[2].wait()
    for c in range(SPANS):
        anchor_v[c * SCEN_L : (c + 1) * SCEN_L, :] = (
            block(prior_v, c) - block(cost_v, c) - block(dual_v, c)
        )
    loads[3].wait()
    highs, lows = [], []
    for c in range(SPANS):
        high, low = split(anchor_v[c * SCEN_L : (c + 1) * SCEN_L, :])
        both = dot_nt(jnp.concatenate([high, low], axis=0), kkt_v[c])
        high, low = split(both[0:SCEN_L] + both[SCEN_L:])
        highs.append(high)
        lows.append(low)
    pick_t = pickt_v[:, 0:ROWS]
    part = dot(pick_t, jnp.concatenate(highs, axis=0)) + dot(pick_t, jnp.concatenate(lows, axis=0))
    sizes = dot(pick_t, jnp.ones((ROWS, BLK), BF16))
    first_high, first_low = split(exp_v[0])
    gathered = [
        jnp.concatenate(
            [half[c // 4 * SCEN_L : (c // 4 + 1) * SCEN_L] for c in range(SPANS)], axis=0
        )
        for half in (first_high, first_low)
    ]
    first_sum = dot(pick_t, gathered[0]) + dot(pick_t, gathered[1])
    place = place_of(lax.broadcasted_iota(jnp.int32, (NODES, BLK), 0))
    group = lax.broadcasted_iota(jnp.int32, (NODES, BLK), 1) >> 5
    extra = jnp.where(group == place, first_sum, 0.0) + jnp.where(
        group == ((place + 2) & 3), sizes, 0.0
    )
    for i in range(NZ):
        rows_i = slice(i * CHUNK, (i + 1) * CHUNK)
        part_v[i, :, 0:K] = part[rows_i]
        part_v[i, :, K:] = extra[rows_i]

    pl.semaphore_wait(barrier, len(Z_OFFS) + len(X_OFFS) + len(A_OFFS) * len(XALL_OFFS))
    send_exports(0)
    for n, off in enumerate(Z_OFFS):
        send(part_v.at[peer_z(off)], rz_v.at[n], zs_sem, zr_sem, {"scen": peer(off)})

    section = jnp.where(my_z < 4, 6, jnp.where(my_z < 6, 5, jnp.where(my_z < 7, 4, 3)))
    slot = jnp.where(my_z < 7, section - 4, 3)

    def echo(c, j):
        wide = dot_nt(kkt_v[c], swh_v[j]) + dot_nt(kkt_v[c], swl_v[j])
        high, low = split(wide)
        return 0.5 * (dot(swh_v[j], high) + dot(swh_v[j], low) + dot(swl_v[j], high))

    gmat_v[0:BLK, :] = echo(section, slot)

    @pl.when(my_z == NZ - 1)
    def _():
        gmat_v[0:BLK, :] += echo(2, 2) + echo(1, 1) + echo(0, 0)

    gmat_v[BLK : BLK + 8, :] = jnp.broadcast_to(left_weight, (8, BLK))
    gmat_v[BLK + 8 :, :] = jnp.broadcast_to(right_weight, (8, BLK))
    send(gmat_v, glow_v, gs_sem.at[0], gr_sem.at[0], {"area": up})
    send(gmat_v, ghigh_v, gs_sem.at[1], gr_sem.at[1], {"area": down})

    first = targets(tie_gap(0))
    exports(lambda c: dot_nt(first[c], kkt_v[c]), 1)
    send_exports(1)

    wait(rz_v, zr_sem)
    acc = part_v[my_z]
    for n in range(len(Z_OFFS)):
        acc = acc + rz_v[n]
    row_c = lax.broadcasted_iota(jnp.int32, (CHUNK, BLK), 0)
    place_c = place_of(row_c + my_z * CHUNK)
    group_c = lax.broadcasted_iota(jnp.int32, (CHUNK, BLK), 1) >> 5
    mine = group_c == place_c
    high, low = split(acc[:, 0:K] * weight3)
    solved = dot(jnp.concatenate([high, low], axis=0), sel_all_v[...])
    solved = jnp.where(mine, solved[0:CHUNK] + solved[CHUNK:], 0.0)
    packed = acc[:, K:] + pltpu.roll(solved, 32, 1)
    block_v[...] = packed
    sumz_v[:, 0:K] = acc[:, 0:K]
    sumz_v[:, K:] = packed
    for k, step in enumerate(A_OFFS):
        for n, off in enumerate(XALL_OFFS):
            send(
                block_v, ra_v.at[k, n], bs_sem, br_sem,
                {"scen": peer(off), "area": area_at(step)},
            )
    for n, off in enumerate(X_OFFS):
        send(sumz_v, rx_v.at[n], xs_sem, xr_sem, {"scen": peer(off)})

    gap = tie_gap(1)
    second = targets(gap)
    for c in range(SPANS):
        current = dot_nt(second[c], kkt_v[c]) * live3
        base = block(dual_v, c) + current
        for b in range(NB):
            base_o[pl.ds(c * NB + b, SCEN_L, stride=STRIDE), :] = base[:, b * BLK : (b + 1) * BLK]

    wait(rx_v, xr_sem)
    wait(ra_v, br_sem)
    wait(glow_v, gr_sem.at[0])
    wait(ghigh_v, gr_sem.at[1])
    acc = sumz_v[...]
    for n in range(len(X_OFFS)):
        acc = acc + rx_v[n]
    packs = {0: acc[:, K:]}
    for k, step in enumerate((2, -2, 1, -1)):
        packs[-step] = (ra_v[k, 0] + ra_v[k, 1]) + (ra_v[k, 2] + ra_v[k, 3])
    first_of = {d: jnp.where(mine, packs[d], 0.0) for d in packs}

    def second_of(d, mat_v):
        left, right = mat_v[BLK : BLK + 1, :], mat_v[BLK + 8 : BLK + 9, :]
        own = first_of[d]
        high, low = split(right * (first_of[d + 1] - own) + left * (first_of[d - 1] - own))
        mat_high, mat_low = split(mat_v[0:BLK, :])
        back = dot_nt(jnp.concatenate([high, low], axis=0), mat_high)
        back = back[0:CHUNK] + back[CHUNK:] + dot_nt(high, mat_low)
        return jnp.where(mine, pltpu.roll(packs[d], BLK - 32, 1) + back, 0.0)

    own = second_of(0, gmat_v)
    gap_sum = right_weight * (second_of(1, ghigh_v) - own) + left_weight * (
        second_of(-1, glow_v) - own
    )
    high, low = split(gap_sum)
    wide = dot(jnp.concatenate([high, low], axis=0), spread_all_v[...])
    high, low = split(0.5 * weight3 * (wide[0:CHUNK] + wide[CHUNK:]))
    both_halves = jnp.concatenate([high, low], axis=0)
    row_k = lax.broadcasted_iota(jnp.int32, (CHUNK, K), 0)

    def solve(c):
        both = dot_nt(both_halves, kkt_v[c])
        return both[0:CHUNK] + both[CHUNK:]

    kgap_v[...] = solve(section)

    @pl.when(my_z == NZ - 1)
    def _():
        found = kgap_v[...]
        for c in (2, 1, 0):
            found = jnp.where(row_k >= BASE[c] - BASE[3], solve(c), found)
        kgap_v[...] = found

    sizes = jnp.max(jnp.where(group_c == ((place_c + 2) & 3), acc[:, K:], 1.0), axis=1, keepdims=True)
    total = (acc[:, 0:K] + kgap_v[...]) / sizes
    total_v[...] = total
    for n, off in enumerate(Z_OFFS):
        send(total_v, gather_v.at[my_z], as_sem, ar_sem.at[n], {"scen": peer(off)})
    gather_v[my_z] = total

    for n, off in enumerate(Z_OFFS):
        source = lax.rem(my_z + NZ - off[1], NZ)
        wait(gather_v.at[source], ar_sem.at[n])
    highs, lows = [], []
    for i in range(NZ):
        high, low = split(gather_v[i])
        highs.append(high)
        lows.append(low)
    averages = jnp.concatenate(highs + lows, axis=0)
    for c in range(SPANS):
        rows_c = slice(c * SCEN_L, (c + 1) * SCEN_L)
        node_mean = dot(pick_v[rows_c, :], averages)
        for b in range(NB):
            place_b = pl.ds(c * NB + b, SCEN_L, stride=STRIDE)
            mean_o[place_b, :] = node_mean[:, b * BLK : (b + 1) * BLK]

    for sweep in range(2):
        wait(exp_v.at[sweep], es_sem.at[sweep, 0])
        wait(exp_v.at[sweep], es_sem.at[sweep, 1])
    wait(rz_v, zs_sem)
    wait(rx_v, xs_sem)
    wait(gather_v.at[0 : NZ - 1], as_sem)
    wait(ra_v, bs_sem)
    wait(gmat_v, gs_sem.at[0])
    wait(gmat_v, gs_sem.at[1])


def on_device(cost_lin, na_dual, prior_mean, kkt_inverse, tie_coef, res_count, line_class, node_of):
    flat = (SCEN_L * STRIDE, BLK)
    hbm = pl.BlockSpec(memory_space=pltpu.HBM)
    vmem = pl.BlockSpec(memory_space=pltpu.VMEM)
    dma = pltpu.SemaphoreType.DMA
    nz, nx = NZ - 1, NX - 1
    scratch = [
        pltpu.VMEM(flat, F32),
        pltpu.VMEM(flat, F32),
        pltpu.VMEM(flat, F32),
        pltpu.VMEM((SPANS, K, K), BF16),
        pltpu.VMEM((BLK, BLK), F32),
        pltpu.VMEM((4, K, BLK), BF16),
        pltpu.VMEM((4, BLK, K), BF16),
        pltpu.VMEM((BLK, K), BF16),
        pltpu.VMEM((ROWS, 2 * BLK), BF16),
        pltpu.VMEM((BLK, K), BF16),
        pltpu.VMEM((ROWS, K), F32),
        pltpu.VMEM((4, BLK, K), BF16),
        pltpu.VMEM((4, BLK, K), BF16),
        pltpu.VMEM((K, BLK), BF16),
        pltpu.VMEM((2, 2 * SCEN_L, BLK), F32),
        pltpu.VMEM((2, 2 * SCEN_L, BLK), F32),
        pltpu.VMEM((2, 2 * SCEN_L, BLK), F32),
        pltpu.VMEM((NZ, CHUNK, WIDE), F32),
        pltpu.VMEM((nz, CHUNK, WIDE), F32),
        pltpu.VMEM((CHUNK, WIDE), F32),
        pltpu.VMEM((nx, CHUNK, WIDE), F32),
        pltpu.VMEM((CHUNK, K), F32),
        pltpu.VMEM((NZ, CHUNK, K), F32),
        pltpu.VMEM((CHUNK, BLK), F32),
        pltpu.VMEM((4, NX, CHUNK, BLK), F32),
        pltpu.VMEM((BLK + 16, BLK), F32),
        pltpu.VMEM((BLK + 16, BLK), F32),
        pltpu.VMEM((BLK + 16, BLK), F32),
        pltpu.VMEM((CHUNK, K), F32),
        dma((4,)), dma((2, 2)), dma((2, 2)), dma, dma, dma, dma, dma, dma((nz,)),
        dma, dma, dma((2,)), dma((2,)),
    ]

    def padded(rows, top):
        return jnp.pad(rows, ((top, 16 - top - rows.shape[0]), (0, BLK - rows.shape[1])))

    small = padded(node_of, 0) + padded(line_class, 9) + padded(res_count.reshape(1, 1), 10)
    small = small.astype(F32) + padded(tie_coef, 8)
    node_mean, base, live = pl.pallas_call(
        kernel,
        out_shape=[jax.ShapeDtypeStruct(flat, F32)] * 2 + [jax.ShapeDtypeStruct((8, BLK), F32)],
        in_specs=[hbm] * 4 + [vmem],
        out_specs=[vmem] * 3,
        scratch_shapes=scratch,
        compiler_params=pltpu.CompilerParams(
            collective_id=0, has_side_effects=True, vmem_limit_bytes=105 * 2**19
        ),
        name="round",
    )(
        cost_lin.reshape(flat), na_dual.reshape(flat), prior_mean.reshape(flat),
        kkt_inverse.reshape(SPANS, K, K), small,
    )
    node_mean = node_mean * live[0:1]
    new_dual = base - node_mean
    return node_mean.reshape(cost_lin.shape), new_dual.reshape(cost_lin.shape)


def solution(mesh):
    placed = (
        P("scen", "area", None, None),
        P("scen", "area", None, None),
        P("scen", "area", None, None),
        P("area", None, None, None),
        P("area", None),
        P("area"),
        P("area", None),
        P(None, "scen"),
    )
    return jax.shard_map(
        on_device,
        mesh=mesh,
        in_specs=placed,
        out_specs=(P("scen", "area", None, None), P("scen", "area", None, None)),
        check_vma=False,
    )
```

```python
import functools

import jax
import jax.numpy as jnp
from jax import lax
from jax.experimental import pallas as pl
from jax.experimental.pallas import tpu as pltpu
from jax.sharding import PartitionSpec as P

F32 = jnp.float32
BF16 = jnp.bfloat16
MESH = pl.DeviceIdType.MESH

SCEN_L = 48
SPANS = 7
K = 384
RES = 16
BLK = 128
NB = K // BLK
ROWS = SCEN_L * SPANS
STRIDE = SPANS * NB
NX, NZ, NA = 4, 8, 16
NODES = 128
CHUNK = NODES // NZ
TILE = NB * CHUNK + 8

BASE = (126, 124, 120, 112, 96, 64, 0)

X_OFFS = ((2, 0), (1, 0), (3, 0))
Z_OFFS = tuple((0, d) for d in (4, 3, 5, 2, 6, 1, 7))
XALL_OFFS = X_OFFS + ((0, 0),)
A_OFFS = (2, NA - 2, 1, NA - 1)


def split(value):
    high = value.astype(BF16)
    low = (value - high.astype(F32)).astype(BF16)
    return high, low


def dot(a, b):
    return jnp.dot(a, b, preferred_element_type=F32)


def dot_nt(a, b):
    return lax.dot_general(a, b, (((1,), (1,)), ((), ())), preferred_element_type=F32)


def kernel(
    cost_h, dual_h, prior_h, kkt_h, small_r,
    mean_o, base_o, live_o,
    cost_v, dual_v, prior_v, kkt_v, node_v, sel_v, spread_v, pick_v, pickt_v,
    anchor_v, swh_v, swl_v, swall_v, sel_all_v, wide_v, wideh_v, widel_v,
    exp_v, low_v, high_v,
    part_v, rz_v, sumz_v, rx_v, total_v, gather_v,
    ra_v, gmat_v, glow_v, ghigh_v,
    in_sem, es_sem, er_sem, zs_sem, zr_sem, xs_sem, xr_sem, as_sem, ar_sem,
    bs_sem, br_sem, gs_sem, gr_sem,
):
    me = lax.axis_index("scen")
    area = lax.axis_index("area")
    my_x = me // NZ
    my_z = lax.rem(me, NZ)
    up = lax.rem(area + 1, NA)
    down = lax.rem(area + NA - 1, NA)

    def peer_z(off):
        return lax.rem(my_z + off[1], NZ)

    def peer(off):
        return lax.rem(my_x + off[0], NX) * NZ + peer_z(off)

    def area_at(step):
        return lax.rem(area + step, NA)

    def send(src, dst, send_sem, recv_sem, device):
        pltpu.make_async_remote_copy(
            src_ref=src, dst_ref=dst, send_sem=send_sem, recv_sem=recv_sem,
            device_id=device, device_id_type=MESH,
        ).start()

    def wait(ref, sem):
        pltpu.make_async_copy(ref, ref, sem).wait()

    loads = [
        pltpu.make_async_copy(src, dst, in_sem.at[i])
        for i, (src, dst) in enumerate(
            ((prior_h, prior_v), (cost_h, cost_v), (dual_h, dual_v), (kkt_h, kkt_v))
        )
    ]
    for load in loads:
        load.start()

    barrier = pltpu.get_barrier_semaphore()
    for off in Z_OFFS + X_OFFS:
        pl.semaphore_signal(barrier, inc=1, device_id={"scen": peer(off)}, device_id_type=MESH)
    for step in A_OFFS:
        for off in XALL_OFFS:
            pl.semaphore_signal(
                barrier, inc=1, device_id={"scen": peer(off), "area": area_at(step)},
                device_id_type=MESH,
            )

    rows = lax.broadcasted_iota(jnp.int32, (K, BLK), 0)
    lanes = lax.broadcasted_iota(jnp.int32, (K, BLK), 1)
    rows_w = lax.broadcasted_iota(jnp.int32, (BLK, K), 0)
    lanes_w = lax.broadcasted_iota(jnp.int32, (BLK, K), 1)
    for j in range(4):
        sel_v[j] = jnp.where(lanes == 32 * j + (rows >> 4), 1.0, 0.0).astype(BF16)
        spread_v[j] = jnp.where(rows_w == 32 * j + (lanes_w >> 4), 1.0, 0.0).astype(BF16)

    small = small_r[8:16, :]
    tie = small
    for shift in (16, 32, 64):
        tie = tie + pltpu.roll(tie, shift, 1)
    lane_row = lax.broadcasted_iota(jnp.int32, (1, BLK), 1)
    live = jnp.where((lane_row & 15).astype(F32) < small[2:3, 0:1], 1.0, 0.0)
    live_o[...] = jnp.broadcast_to(live, (8, BLK))
    weight = tie[0:1] * live
    live3 = jnp.concatenate([live] * NB, axis=1)
    weight3 = jnp.concatenate([weight] * NB, axis=1)
    for j in range(4):
        placed = jnp.where(rows_w == 32 * j + (lanes_w >> 4), 1.0, 0.0)
        swh_v[j], swl_v[j] = split(placed * weight3)
    swall_v[0], swall_v[1] = split(jnp.where((rows_w & 31) == (lanes_w >> 4), 1.0, 0.0) * weight3)
    sel_all_v[...] = jnp.where((lanes & 31) == (rows >> 4), 1.0, 0.0).astype(BF16)
    left_weight = jnp.broadcast_to(small[1:2, 0:1], (1, BLK)) / 3.0
    right_weight = jnp.broadcast_to(small[1:2, 1:2], (1, BLK)) / 3.0

    node_v[...] = jnp.zeros((BLK, BLK), F32)
    node_v[0:8, :] = small_r[0:8, :]
    node_t = jnp.transpose(node_v[...])
    node_lane = lax.broadcasted_iota(jnp.int32, (SCEN_L, BLK), 1).astype(F32)
    picks = []
    for c in range(SPANS):
        picks.append(jnp.where(node_lane - BASE[c] == node_t[0:SCEN_L, c : c + 1], 1.0, 0.0))
    picks.append(jnp.zeros((K - ROWS, BLK), F32))
    pick = jnp.concatenate(picks, axis=0)
    pickt_v[...] = jnp.transpose(pick).astype(BF16)
    pick_b = pick[0:ROWS].astype(BF16)
    pick_v[:, 0:BLK] = pick_b
    pick_v[:, BLK:] = pick_b

    def place_of(row):
        place = jnp.where(row < 64, 2, jnp.where(row < 96, 1, 0))
        place = jnp.where(row >= 112, 3, place)
        place = jnp.where(row >= 120, 2, place)
        place = jnp.where(row >= 124, 1, place)
        return jnp.where(row >= 126, 0, place)

    def block(ref, c):
        return jnp.concatenate(
            [ref[pl.ds(c * NB + b, SCEN_L, stride=STRIDE), :] for b in range(NB)], axis=1
        )

    def exports(value_of, sweep):
        groups = [None, None]
        for c in range(SPANS):
            g, j = c // 4, c % 4
            high, low = split(value_of(c) * weight3)
            part = dot(jnp.concatenate([high, low], axis=0), sel_v[j])
            part = part[0:SCEN_L] + part[SCEN_L:]
            groups[g] = part if groups[g] is None else groups[g] + part
        exp_v[sweep] = jnp.concatenate(groups, axis=0)

    def send_exports(sweep):
        send(exp_v.at[sweep], low_v.at[sweep], es_sem.at[sweep, 0], er_sem.at[sweep, 0], {"area": up})
        send(exp_v.at[sweep], high_v.at[sweep], es_sem.at[sweep, 1], er_sem.at[sweep, 1], {"area": down})

    def tie_gap(sweep):
        wait(low_v.at[sweep], er_sem.at[sweep, 0])
        wait(high_v.at[sweep], er_sem.at[sweep, 1])
        own = exp_v[sweep]
        return right_weight * (high_v[sweep] - own) + left_weight * (low_v[sweep] - own)

    def targets(gap):
        high, low = split(gap)
        found = []
        for c in range(SPANS):
            g, j = c // 4, c % 4
            rows_g = slice(g * SCEN_L, (g + 1) * SCEN_L)
            wide = dot(jnp.concatenate([high[rows_g], low[rows_g]], axis=0), spread_v[j])
            coupling = 0.5 * weight3 * (wide[0:SCEN_L] + wide[SCEN_L:])
            found.append((anchor_v[c * SCEN_L : (c + 1) * SCEN_L, :] + coupling).astype(BF16))
        return found

    loads[0].wait()
    exports(lambda c: block(prior_v, c), 0)

    loads[1].wait()
    loads[2].wait()
    for c in range(SPANS):
        anchor_v[c * SCEN_L : (c + 1) * SCEN_L, :] = (
            block(prior_v, c) - block(cost_v, c) - block(dual_v, c)
        )
    loads[3].wait()
    highs, lows = [], []
    for c in range(SPANS):
        high, low = split(anchor_v[c * SCEN_L : (c + 1) * SCEN_L, :])
        both = dot_nt(jnp.concatenate([high, low], axis=0), kkt_v[c])
        high, low = split(both[0:SCEN_L] + both[SCEN_L:])
        highs.append(high)
        lows.append(low)
    pick_t = pickt_v[:, 0:ROWS]
    part = dot(pick_t, jnp.concatenate(highs, axis=0)) + dot(pick_t, jnp.concatenate(lows, axis=0))
    sizes = dot(pick_t, jnp.ones((ROWS, BLK), BF16))
    first_high, first_low = split(exp_v[0])
    gathered = [
        jnp.concatenate(
            [half[c // 4 * SCEN_L : (c // 4 + 1) * SCEN_L] for c in range(SPANS)], axis=0
        )
        for half in (first_high, first_low)
    ]
    first_sum = dot(pick_t, gathered[0]) + dot(pick_t, gathered[1])
    place = place_of(lax.broadcasted_iota(jnp.int32, (NODES, BLK), 0))
    group = lax.broadcasted_iota(jnp.int32, (NODES, BLK), 1) >> 5
    high, low = split(part * weight3)
    solved = dot(jnp.concatenate([high, low], axis=0), sel_all_v[...])
    solved = solved[0:NODES] + solved[NODES:]
    in_row = jnp.where(group == place, first_sum, 0.0)
    in_row = in_row + pltpu.roll(in_row, 32, 1)
    in_row = in_row + pltpu.roll(in_row, 64, 1)
    lane_n = lax.broadcasted_iota(jnp.int32, (NODES, BLK), 1) & 31
    in_row = jnp.where(lane_n >= 24, sizes, in_row)
    group_8 = lax.broadcasted_iota(jnp.int32, (8, BLK), 1) >> 5
    for i in range(NZ):
        top = slice(i * CHUNK, i * CHUNK + 8)
        low_half = slice(i * CHUNK + 8, (i + 1) * CHUNK)
        for b in range(NB):
            part_v[i, b * CHUNK : (b + 1) * CHUNK, :] = part[
                i * CHUNK : (i + 1) * CHUNK, b * BLK : (b + 1) * BLK
            ]
        packed = jnp.where(group_8 == 0, in_row[top], solved[top])
        packed = jnp.where(group_8 == 2, in_row[low_half], packed)
        part_v[i, NB * CHUNK :, :] = jnp.where(group_8 == 3, solved[low_half], packed)

    pl.semaphore_wait(barrier, len(Z_OFFS) + len(X_OFFS) + len(A_OFFS) * len(XALL_OFFS))
    send_exports(0)
    for n, off in enumerate(Z_OFFS):
        send(part_v.at[peer_z(off)], rz_v.at[n], zs_sem, zr_sem, {"scen": peer(off)})

    section = jnp.where(my_z < 4, 6, jnp.where(my_z < 6, 5, jnp.where(my_z < 7, 4, 3)))
    slot = jnp.where(my_z < 7, section - 4, 3)

    def response(c, j):
        return dot_nt(kkt_v[c], swh_v[j]) + dot_nt(kkt_v[c], swl_v[j])

    wide_v[...] = response(section, slot)

    @pl.when(my_z == NZ - 1)
    def _():
        wide_v[...] += response(2, 2) + response(1, 1) + response(0, 0)

    high, low = split(0.5 * wide_v[...])
    wideh_v[...] = high
    widel_v[...] = low
    back = dot(swall_v[0], high) + dot(swall_v[0], low) + dot(swall_v[1], high)
    row_g = lax.broadcasted_iota(jnp.int32, (BLK, BLK), 0) >> 5
    lane_g = lax.broadcasted_iota(jnp.int32, (BLK, BLK), 1) >> 5
    gmat_v[0:BLK, :] = jnp.where(row_g == lane_g, back, 0.0)
    gmat_v[BLK : BLK + 8, :] = jnp.broadcast_to(left_weight, (8, BLK))
    gmat_v[BLK + 8 :, :] = jnp.broadcast_to(right_weight, (8, BLK))
    send(gmat_v, glow_v, gs_sem.at[0], gr_sem.at[0], {"area": up})
    send(gmat_v, ghigh_v, gs_sem.at[1], gr_sem.at[1], {"area": down})

    wait(rz_v, zr_sem)
    acc = part_v[my_z]
    for n in range(len(Z_OFFS)):
        acc = acc + rz_v[n]
    row_c = lax.broadcasted_iota(jnp.int32, (CHUNK, BLK), 0)
    place_c = place_of(row_c + my_z * CHUNK)
    group_c = lax.broadcasted_iota(jnp.int32, (CHUNK, BLK), 1) >> 5
    mine = group_c == place_c
    sumz_v[...] = acc
    for n, off in enumerate(X_OFFS):
        send(sumz_v, rx_v.at[n], xs_sem, xr_sem, {"scen": peer(off)})
    for k, step in enumerate(A_OFFS):
        for n, off in enumerate(XALL_OFFS):
            send(
                sumz_v.at[NB * CHUNK :], ra_v.at[k, n], bs_sem, br_sem,
                {"scen": peer(off), "area": area_at(step)},
            )

    first = targets(tie_gap(0))
    exports(lambda c: dot_nt(first[c], kkt_v[c]), 1)
    send_exports(1)

    wait(glow_v, gr_sem.at[0])
    wait(ghigh_v, gr_sem.at[1])
    mats = jnp.concatenate([ghigh_v[0:BLK, :], glow_v[0:BLK, :], gmat_v[0:BLK, :]], axis=1)
    mats_high, mats_low = split(mats)
    wait(rx_v, xr_sem)
    wait(ra_v, br_sem)
    acc = sumz_v[...]
    for n in range(len(X_OFFS)):
        acc = acc + rx_v[n]
    solved = jnp.concatenate([acc[b * CHUNK : (b + 1) * CHUNK] for b in range(NB)], axis=1)
    packs = {0: acc[NB * CHUNK :]}
    for k, step in enumerate((2, -2, 1, -1)):
        packs[-step] = (ra_v[k, 0] + ra_v[k, 1]) + (ra_v[k, 2] + ra_v[k, 3])

    def unpack(packed, first):
        halves = []
        for g in (first, first + 2):
            value = jnp.where(group_8 == g, packed, 0.0)
            value = value + pltpu.roll(value, 32, 1)
            halves.append(value + pltpu.roll(value, 64, 1))
        return jnp.concatenate(halves, axis=0)

    own = unpack(packs[0], 0)

    def first_gap(d, mat_v):
        left, right = mat_v[BLK : BLK + 1, :], mat_v[BLK + 8 : BLK + 9, :]
        gap_d = right * (packs[d + 1] - packs[d]) + left * (packs[d - 1] - packs[d])
        return jnp.where(mine, unpack(gap_d, 0), 0.0)

    both_weights = left_weight + right_weight
    gaps = jnp.concatenate(
        [
            right_weight * first_gap(1, ghigh_v),
            left_weight * first_gap(-1, glow_v),
            -both_weights * first_gap(0, gmat_v),
        ],
        axis=1,
    )
    high, low = split(gaps)
    back = dot_nt(jnp.concatenate([high, low], axis=0), mats_high)
    back = back[0:CHUNK] + back[CHUNK:] + dot_nt(high, mats_low)
    anchor_gap = right_weight * (packs[1] - packs[0]) + left_weight * (packs[-1] - packs[0])
    gap_sum = jnp.where(mine, unpack(anchor_gap, 1) + back, 0.0)
    high, low = split(gap_sum)
    kgap = dot_nt(jnp.concatenate([high, low], axis=0), wideh_v[...])
    kgap = kgap[0:CHUNK] + kgap[CHUNK:] + dot_nt(high, widel_v[...])

    lane_c = lax.broadcasted_iota(jnp.int32, (CHUNK, BLK), 1) & 31
    sizes = jnp.max(jnp.where(lane_c >= 24, own, 1.0), axis=1, keepdims=True)
    total = (solved + kgap) / sizes
    total_v[...] = total
    for n, off in enumerate(Z_OFFS):
        send(total_v, gather_v.at[my_z], as_sem, ar_sem.at[n], {"scen": peer(off)})
    gather_v[my_z] = total

    gap = tie_gap(1)
    second = targets(gap)
    for c in range(SPANS):
        current = dot_nt(second[c], kkt_v[c]) * live3
        base = block(dual_v, c) + current
        for b in range(NB):
            base_o[pl.ds(c * NB + b, SCEN_L, stride=STRIDE), :] = base[:, b * BLK : (b + 1) * BLK]

    for n, off in enumerate(Z_OFFS):
        source = lax.rem(my_z + NZ - off[1], NZ)
        wait(gather_v.at[source], ar_sem.at[n])
    highs, lows = [], []
    for i in range(NZ):
        high, low = split(gather_v[i])
        highs.append(high)
        lows.append(low)
    averages = jnp.concatenate(highs + lows, axis=0)
    for c in range(SPANS):
        rows_c = slice(c * SCEN_L, (c + 1) * SCEN_L)
        node_mean = dot(pick_v[rows_c, :], averages)
        for b in range(NB):
            place_b = pl.ds(c * NB + b, SCEN_L, stride=STRIDE)
            mean_o[place_b, :] = node_mean[:, b * BLK : (b + 1) * BLK]

    for sweep in range(2):
        wait(exp_v.at[sweep], es_sem.at[sweep, 0])
        wait(exp_v.at[sweep], es_sem.at[sweep, 1])
    wait(rz_v, zs_sem)
    wait(rx_v, xs_sem)
    wait(gather_v.at[0 : NZ - 1], as_sem)
    wait(ra_v, bs_sem)
    wait(gmat_v, gs_sem.at[0])
    wait(gmat_v, gs_sem.at[1])


def on_device(cost_lin, na_dual, prior_mean, kkt_inverse, tie_coef, res_count, line_class, node_of):
    flat = (SCEN_L * STRIDE, BLK)
    hbm = pl.BlockSpec(memory_space=pltpu.HBM)
    vmem = pl.BlockSpec(memory_space=pltpu.VMEM)
    dma = pltpu.SemaphoreType.DMA
    nz, nx = NZ - 1, NX - 1
    scratch = [
        pltpu.VMEM(flat, F32),
        pltpu.VMEM(flat, F32),
        pltpu.VMEM(flat, F32),
        pltpu.VMEM((SPANS, K, K), BF16),
        pltpu.VMEM((BLK, BLK), F32),
        pltpu.VMEM((4, K, BLK), BF16),
        pltpu.VMEM((4, BLK, K), BF16),
        pltpu.VMEM((ROWS, 2 * BLK), BF16),
        pltpu.VMEM((BLK, K), BF16),
        pltpu.VMEM((ROWS, K), F32),
        pltpu.VMEM((4, BLK, K), BF16),
        pltpu.VMEM((4, BLK, K), BF16),
        pltpu.VMEM((2, BLK, K), BF16),
        pltpu.VMEM((K, BLK), BF16),
        pltpu.VMEM((K, BLK), F32),
        pltpu.VMEM((K, BLK), BF16),
        pltpu.VMEM((K, BLK), BF16),
        pltpu.VMEM((2, 2 * SCEN_L, BLK), F32),
        pltpu.VMEM((2, 2 * SCEN_L, BLK), F32),
        pltpu.VMEM((2, 2 * SCEN_L, BLK), F32),
        pltpu.VMEM((NZ, TILE, BLK), F32),
        pltpu.VMEM((nz, TILE, BLK), F32),
        pltpu.VMEM((TILE, BLK), F32),
        pltpu.VMEM((nx, TILE, BLK), F32),
        pltpu.VMEM((CHUNK, K), F32),
        pltpu.VMEM((NZ, CHUNK, K), F32),
        pltpu.VMEM((4, NX, 8, BLK), F32),
        pltpu.VMEM((BLK + 16, BLK), F32),
        pltpu.VMEM((BLK + 16, BLK), F32),
        pltpu.VMEM((BLK + 16, BLK), F32),
        dma((4,)), dma((2, 2)), dma((2, 2)), dma, dma, dma, dma, dma, dma((nz,)),
        dma, dma, dma((2,)), dma((2,)),
    ]

    def padded(rows, top):
        return jnp.pad(rows, ((top, 16 - top - rows.shape[0]), (0, BLK - rows.shape[1])))

    small = padded(node_of, 0) + padded(line_class, 9) + padded(res_count.reshape(1, 1), 10)
    small = small.astype(F32) + padded(tie_coef, 8)
    node_mean, base, live = pl.pallas_call(
        kernel,
        out_shape=[jax.ShapeDtypeStruct(flat, F32)] * 2 + [jax.ShapeDtypeStruct((8, BLK), F32)],
        in_specs=[hbm] * 4 + [vmem],
        out_specs=[vmem] * 3,
        scratch_shapes=scratch,
        compiler_params=pltpu.CompilerParams(
            collective_id=0, has_side_effects=True, vmem_limit_bytes=105 * 2**19
        ),
        name="round",
    )(
        cost_lin.reshape(flat), na_dual.reshape(flat), prior_mean.reshape(flat),
        kkt_inverse.reshape(SPANS, K, K), small,
    )
    node_mean = node_mean * live[0:1]
    new_dual = base - node_mean
    return node_mean.reshape(cost_lin.shape), new_dual.reshape(cost_lin.shape)


def solution(mesh):
    placed = (
        P("scen", "area", None, None),
        P("scen", "area", None, None),
        P("scen", "area", None, None),
        P("area", None, None, None),
        P("area", None),
        P("area"),
        P("area", None),
        P(None, "scen"),
    )
    return jax.shard_map(
        on_device,
        mesh=mesh,
        in_specs=placed,
        out_specs=(P("scen", "area", None, None), P("scen", "area", None, None)),
        check_vma=False,
    )
```

```python
import functools

import jax
import jax.numpy as jnp
from jax import lax
from jax.experimental import pallas as pl
from jax.experimental.pallas import tpu as pltpu
from jax.sharding import PartitionSpec as P

F32 = jnp.float32
BF16 = jnp.bfloat16
MESH = pl.DeviceIdType.MESH

SCEN_L = 48
SPANS = 7
K = 384
RES = 16
BLK = 128
NB = K // BLK
ROWS = SCEN_L * SPANS
STRIDE = SPANS * NB
NX, NZ, NA = 4, 8, 16
NODES = 128
CHUNK = NODES // NZ
TILE = NB * CHUNK + 8

BASE = (126, 124, 120, 112, 96, 64, 0)

X_OFFS = ((2, 0), (1, 0), (3, 0))
Z_OFFS = tuple((0, d) for d in (4, 3, 5, 2, 6, 1, 7))
XALL_OFFS = X_OFFS + ((0, 0),)
A_OFFS = (2, NA - 2, 1, NA - 1)


def split(value):
    high = value.astype(BF16)
    low = (value - high.astype(F32)).astype(BF16)
    return high, low


def dot(a, b):
    return jnp.dot(a, b, preferred_element_type=F32)


def dot_nt(a, b):
    return lax.dot_general(a, b, (((1,), (1,)), ((), ())), preferred_element_type=F32)


def kernel(
    cost_h, dual_h, prior_h, kkt_h, small_r,
    mean_o, base_o, live_o,
    cost_v, dual_v, prior_v, kkt_v, node_v, sel_v, spread_v, pick_v, pickt_v,
    anchor_v, swh_v, swl_v, swall_v, sel_all_v, wide_v, wideh_v, widel_v,
    exp_v, low_v, high_v,
    part_v, rz_v, sumz_v, rx_v, total_v, gather_v,
    ra_v, gmat_v, glow_v, ghigh_v,
    in_sem, es_sem, er_sem, zs_sem, zr_sem, xs_sem, xr_sem, as_sem, ar_sem,
    bs_sem, br_sem, gs_sem, gr_sem,
):
    me = lax.axis_index("scen")
    area = lax.axis_index("area")
    my_x = me // NZ
    my_z = lax.rem(me, NZ)
    up = lax.rem(area + 1, NA)
    down = lax.rem(area + NA - 1, NA)

    def peer_z(off):
        return lax.rem(my_z + off[1], NZ)

    def peer(off):
        return lax.rem(my_x + off[0], NX) * NZ + peer_z(off)

    def area_at(step):
        return lax.rem(area + step, NA)

    def send(src, dst, send_sem, recv_sem, device):
        pltpu.make_async_remote_copy(
            src_ref=src, dst_ref=dst, send_sem=send_sem, recv_sem=recv_sem,
            device_id=device, device_id_type=MESH,
        ).start()

    def wait(ref, sem):
        pltpu.make_async_copy(ref, ref, sem).wait()

    loads = [
        pltpu.make_async_copy(src, dst, in_sem.at[i])
        for i, (src, dst) in enumerate(
            ((prior_h, prior_v), (cost_h, cost_v), (dual_h, dual_v), (kkt_h, kkt_v))
        )
    ]
    for load in loads:
        load.start()

    barrier = pltpu.get_barrier_semaphore()
    for off in Z_OFFS + X_OFFS:
        pl.semaphore_signal(barrier, inc=1, device_id={"scen": peer(off)}, device_id_type=MESH)
    for step in A_OFFS:
        for off in XALL_OFFS:
            pl.semaphore_signal(
                barrier, inc=1, device_id={"scen": peer(off), "area": area_at(step)},
                device_id_type=MESH,
            )

    rows = lax.broadcasted_iota(jnp.int32, (K, BLK), 0)
    lanes = lax.broadcasted_iota(jnp.int32, (K, BLK), 1)
    rows_w = lax.broadcasted_iota(jnp.int32, (BLK, K), 0)
    lanes_w = lax.broadcasted_iota(jnp.int32, (BLK, K), 1)
    for j in range(4):
        sel_v[j] = jnp.where(lanes == 32 * j + (rows >> 4), 1.0, 0.0).astype(BF16)
        spread_v[j] = jnp.where(rows_w == 32 * j + (lanes_w >> 4), 1.0, 0.0).astype(BF16)

    small = small_r[8:16, :]
    tie = small
    for shift in (16, 32, 64):
        tie = tie + pltpu.roll(tie, shift, 1)
    lane_row = lax.broadcasted_iota(jnp.int32, (1, BLK), 1)
    live = jnp.where((lane_row & 15).astype(F32) < small[2:3, 0:1], 1.0, 0.0)
    live_o[...] = jnp.broadcast_to(live, (8, BLK))
    weight = tie[0:1] * live
    live3 = jnp.concatenate([live] * NB, axis=1)
    weight3 = jnp.concatenate([weight] * NB, axis=1)
    for j in range(4):
        placed = jnp.where(rows_w == 32 * j + (lanes_w >> 4), 1.0, 0.0)
        swh_v[j], swl_v[j] = split(placed * weight3)
    swall_v[0], swall_v[1] = split(jnp.where((rows_w & 31) == (lanes_w >> 4), 1.0, 0.0) * weight3)
    sel_all_v[...] = jnp.where((lanes & 31) == (rows >> 4), 1.0, 0.0).astype(BF16)
    left_weight = jnp.broadcast_to(small[1:2, 0:1], (1, BLK)) / 3.0
    right_weight = jnp.broadcast_to(small[1:2, 1:2], (1, BLK)) / 3.0

    node_v[...] = jnp.zeros((BLK, BLK), F32)
    node_v[0:8, :] = small_r[0:8, :]
    node_t = jnp.transpose(node_v[...])
    node_lane = lax.broadcasted_iota(jnp.int32, (SCEN_L, BLK), 1).astype(F32)
    picks = []
    for c in range(SPANS):
        picks.append(jnp.where(node_lane - BASE[c] == node_t[0:SCEN_L, c : c + 1], 1.0, 0.0))
    picks.append(jnp.zeros((K - ROWS, BLK), F32))
    pick = jnp.concatenate(picks, axis=0)
    pickt_v[...] = jnp.transpose(pick).astype(BF16)
    pick_b = pick[0:ROWS].astype(BF16)
    pick_v[:, 0:BLK] = pick_b
    pick_v[:, BLK:] = pick_b

    def place_of(row):
        place = jnp.where(row < 64, 2, jnp.where(row < 96, 1, 0))
        place = jnp.where(row >= 112, 3, place)
        place = jnp.where(row >= 120, 2, place)
        place = jnp.where(row >= 124, 1, place)
        return jnp.where(row >= 126, 0, place)

    def block(ref, c):
        return jnp.concatenate(
            [ref[pl.ds(c * NB + b, SCEN_L, stride=STRIDE), :] for b in range(NB)], axis=1
        )

    def exports(value_of, sweep):
        groups = [None, None]
        for c in range(SPANS):
            g, j = c // 4, c % 4
            high, low = split(value_of(c) * weight3)
            part = dot(jnp.concatenate([high, low], axis=0), sel_v[j])
            part = part[0:SCEN_L] + part[SCEN_L:]
            groups[g] = part if groups[g] is None else groups[g] + part
        exp_v[sweep] = jnp.concatenate(groups, axis=0)

    def send_exports(sweep):
        send(exp_v.at[sweep], low_v.at[sweep], es_sem.at[sweep, 0], er_sem.at[sweep, 0], {"area": up})
        send(exp_v.at[sweep], high_v.at[sweep], es_sem.at[sweep, 1], er_sem.at[sweep, 1], {"area": down})

    def tie_gap(sweep):
        wait(low_v.at[sweep], er_sem.at[sweep, 0])
        wait(high_v.at[sweep], er_sem.at[sweep, 1])
        own = exp_v[sweep]
        return right_weight * (high_v[sweep] - own) + left_weight * (low_v[sweep] - own)

    def targets(gap):
        high, low = split(gap)
        found = []
        for c in range(SPANS):
            g, j = c // 4, c % 4
            rows_g = slice(g * SCEN_L, (g + 1) * SCEN_L)
            wide = dot(jnp.concatenate([high[rows_g], low[rows_g]], axis=0), spread_v[j])
            coupling = 0.5 * weight3 * (wide[0:SCEN_L] + wide[SCEN_L:])
            found.append((anchor_v[c * SCEN_L : (c + 1) * SCEN_L, :] + coupling).astype(BF16))
        return found

    loads[0].wait()
    exports(lambda c: block(prior_v, c), 0)

    loads[1].wait()
    loads[2].wait()
    for c in range(SPANS):
        anchor_v[c * SCEN_L : (c + 1) * SCEN_L, :] = (
            block(prior_v, c) - block(cost_v, c) - block(dual_v, c)
        )
    loads[3].wait()
    highs, lows = [], []
    for c in range(SPANS):
        high, low = split(anchor_v[c * SCEN_L : (c + 1) * SCEN_L, :])
        both = dot_nt(jnp.concatenate([high, low], axis=0), kkt_v[c])
        high, low = split(both[0:SCEN_L] + both[SCEN_L:])
        highs.append(high)
        lows.append(low)
    pick_t = pickt_v[:, 0:ROWS]
    part = dot(pick_t, jnp.concatenate(highs, axis=0)) + dot(pick_t, jnp.concatenate(lows, axis=0))
    sizes = dot(pick_t, jnp.ones((ROWS, BLK), BF16))
    first_high, first_low = split(exp_v[0])
    gathered = [
        jnp.concatenate(
            [half[c // 4 * SCEN_L : (c // 4 + 1) * SCEN_L] for c in range(SPANS)], axis=0
        )
        for half in (first_high, first_low)
    ]
    first_sum = dot(pick_t, gathered[0]) + dot(pick_t, gathered[1])
    place = place_of(lax.broadcasted_iota(jnp.int32, (NODES, BLK), 0))
    group = lax.broadcasted_iota(jnp.int32, (NODES, BLK), 1) >> 5
    high, low = split(part * weight3)
    solved = dot(jnp.concatenate([high, low], axis=0), sel_all_v[...])
    solved = solved[0:NODES] + solved[NODES:]
    in_row = jnp.where(group == place, first_sum, 0.0)
    in_row = in_row + pltpu.roll(in_row, 32, 1)
    in_row = in_row + pltpu.roll(in_row, 64, 1)
    lane_n = lax.broadcasted_iota(jnp.int32, (NODES, BLK), 1) & 31
    in_row = jnp.where(lane_n >= 24, sizes, in_row)
    group_8 = lax.broadcasted_iota(jnp.int32, (8, BLK), 1) >> 5
    for i in range(NZ):
        top = slice(i * CHUNK, i * CHUNK + 8)
        low_half = slice(i * CHUNK + 8, (i + 1) * CHUNK)
        for b in range(NB):
            part_v[i, b * CHUNK : (b + 1) * CHUNK, :] = part[
                i * CHUNK : (i + 1) * CHUNK, b * BLK : (b + 1) * BLK
            ]
        packed = jnp.where(group_8 == 0, in_row[top], solved[top])
        packed = jnp.where(group_8 == 2, in_row[low_half], packed)
        part_v[i, NB * CHUNK :, :] = jnp.where(group_8 == 3, solved[low_half], packed)

    pl.semaphore_wait(barrier, len(Z_OFFS) + len(X_OFFS) + len(A_OFFS) * len(XALL_OFFS))
    send_exports(0)
    for n, off in enumerate(Z_OFFS):
        send(part_v.at[peer_z(off)], rz_v.at[n], zs_sem, zr_sem, {"scen": peer(off)})

    section = jnp.where(my_z < 4, 6, jnp.where(my_z < 6, 5, jnp.where(my_z < 7, 4, 3)))
    slot = jnp.where(my_z < 7, section - 4, 3)

    def response(c, j):
        return dot_nt(kkt_v[c], swh_v[j]) + dot_nt(kkt_v[c], swl_v[j])

    wide_v[...] = response(section, slot)

    @pl.when(my_z == NZ - 1)
    def _():
        wide_v[...] += response(2, 2) + response(1, 1) + response(0, 0)

    high, low = split(0.5 * wide_v[...])
    wideh_v[...] = high
    widel_v[...] = low
    back = dot(swall_v[0], high) + dot(swall_v[0], low) + dot(swall_v[1], high)
    row_g = lax.broadcasted_iota(jnp.int32, (BLK, BLK), 0) >> 5
    lane_g = lax.broadcasted_iota(jnp.int32, (BLK, BLK), 1) >> 5
    gmat_v[0:BLK, :] = jnp.where(row_g == lane_g, back, 0.0)
    gmat_v[BLK : BLK + 8, :] = jnp.broadcast_to(left_weight, (8, BLK))
    gmat_v[BLK + 8 :, :] = jnp.broadcast_to(right_weight, (8, BLK))
    send(gmat_v, glow_v, gs_sem.at[0], gr_sem.at[0], {"area": up})
    send(gmat_v, ghigh_v, gs_sem.at[1], gr_sem.at[1], {"area": down})

    wait(rz_v, zr_sem)
    acc = part_v[my_z]
    for n in range(len(Z_OFFS)):
        acc = acc + rz_v[n]
    row_c = lax.broadcasted_iota(jnp.int32, (CHUNK, BLK), 0)
    place_c = place_of(row_c + my_z * CHUNK)
    group_c = lax.broadcasted_iota(jnp.int32, (CHUNK, BLK), 1) >> 5
    mine = group_c == place_c
    sumz_v[...] = acc
    for k, step in enumerate(A_OFFS):
        for n, off in enumerate(XALL_OFFS):
            send(
                sumz_v.at[NB * CHUNK :], ra_v.at[k, n], bs_sem, br_sem,
                {"scen": peer(off), "area": area_at(step)},
            )
    for n, off in enumerate(X_OFFS):
        send(sumz_v, rx_v.at[n], xs_sem, xr_sem, {"scen": peer(off)})

    first = targets(tie_gap(0))
    exports(lambda c: dot_nt(first[c], kkt_v[c]), 1)
    send_exports(1)

    wait(glow_v, gr_sem.at[0])
    wait(ghigh_v, gr_sem.at[1])
    mats = jnp.concatenate([ghigh_v[0:BLK, :], glow_v[0:BLK, :], gmat_v[0:BLK, :]], axis=1)
    mats_high, mats_low = split(mats)
    wait(rx_v, xr_sem)
    wait(ra_v, br_sem)
    acc = sumz_v[...]
    for n in range(len(X_OFFS)):
        acc = acc + rx_v[n]
    solved = jnp.concatenate([acc[b * CHUNK : (b + 1) * CHUNK] for b in range(NB)], axis=1)
    packs = {0: acc[NB * CHUNK :]}
    for k, step in enumerate((2, -2, 1, -1)):
        packs[-step] = (ra_v[k, 0] + ra_v[k, 1]) + (ra_v[k, 2] + ra_v[k, 3])

    def unpack(packed, first):
        halves = []
        for g in (first, first + 2):
            value = jnp.where(group_8 == g, packed, 0.0)
            value = value + pltpu.roll(value, 32, 1)
            halves.append(value + pltpu.roll(value, 64, 1))
        return jnp.concatenate(halves, axis=0)

    own = unpack(packs[0], 0)

    def first_gap(d, mat_v):
        left, right = mat_v[BLK : BLK + 1, :], mat_v[BLK + 8 : BLK + 9, :]
        gap_d = right * (packs[d + 1] - packs[d]) + left * (packs[d - 1] - packs[d])
        return jnp.where(mine, unpack(gap_d, 0), 0.0)

    both_weights = left_weight + right_weight
    gaps = jnp.concatenate(
        [
            right_weight * first_gap(1, ghigh_v),
            left_weight * first_gap(-1, glow_v),
            -both_weights * first_gap(0, gmat_v),
        ],
        axis=1,
    )
    high, low = split(gaps)
    back = dot_nt(jnp.concatenate([high, low], axis=0), mats_high)
    back = back[0:CHUNK] + back[CHUNK:] + dot_nt(high, mats_low)
    anchor_gap = right_weight * (packs[1] - packs[0]) + left_weight * (packs[-1] - packs[0])
    gap_sum = jnp.where(mine, unpack(anchor_gap, 1) + back, 0.0)
    high, low = split(gap_sum)
    kgap = dot_nt(jnp.concatenate([high, low], axis=0), wideh_v[...])
    kgap = kgap[0:CHUNK] + kgap[CHUNK:] + dot_nt(high, widel_v[...])

    lane_c = lax.broadcasted_iota(jnp.int32, (CHUNK, BLK), 1) & 31
    sizes = jnp.max(jnp.where(lane_c >= 24, own, 1.0), axis=1, keepdims=True)
    total = (solved + kgap) / sizes
    total_v[...] = total
    for n, off in enumerate(Z_OFFS):
        send(total_v, gather_v.at[my_z], as_sem, ar_sem.at[n], {"scen": peer(off)})
    gather_v[my_z] = total

    gap = tie_gap(1)
    second = targets(gap)
    for c in range(SPANS):
        current = dot_nt(second[c], kkt_v[c]) * live3
        base = block(dual_v, c) + current
        for b in range(NB):
            base_o[pl.ds(c * NB + b, SCEN_L, stride=STRIDE), :] = base[:, b * BLK : (b + 1) * BLK]

    for n, off in enumerate(Z_OFFS):
        source = lax.rem(my_z + NZ - off[1], NZ)
        wait(gather_v.at[source], ar_sem.at[n])
    highs, lows = [], []
    for i in range(NZ):
        high, low = split(gather_v[i])
        highs.append(high)
        lows.append(low)
    averages = jnp.concatenate(highs + lows, axis=0)
    for c in range(SPANS):
        rows_c = slice(c * SCEN_L, (c + 1) * SCEN_L)
        node_mean = dot(pick_v[rows_c, :], averages)
        for b in range(NB):
            place_b = pl.ds(c * NB + b, SCEN_L, stride=STRIDE)
            mean_o[place_b, :] = node_mean[:, b * BLK : (b + 1) * BLK]

    for sweep in range(2):
        wait(exp_v.at[sweep], es_sem.at[sweep, 0])
        wait(exp_v.at[sweep], es_sem.at[sweep, 1])
    wait(rz_v, zs_sem)
    wait(rx_v, xs_sem)
    wait(gather_v.at[0 : NZ - 1], as_sem)
    wait(ra_v, bs_sem)
    wait(gmat_v, gs_sem.at[0])
    wait(gmat_v, gs_sem.at[1])


def on_device(cost_lin, na_dual, prior_mean, kkt_inverse, tie_coef, res_count, line_class, node_of):
    flat = (SCEN_L * STRIDE, BLK)
    hbm = pl.BlockSpec(memory_space=pltpu.HBM)
    vmem = pl.BlockSpec(memory_space=pltpu.VMEM)
    dma = pltpu.SemaphoreType.DMA
    nz, nx = NZ - 1, NX - 1
    scratch = [
        pltpu.VMEM(flat, F32),
        pltpu.VMEM(flat, F32),
        pltpu.VMEM(flat, F32),
        pltpu.VMEM((SPANS, K, K), BF16),
        pltpu.VMEM((BLK, BLK), F32),
        pltpu.VMEM((4, K, BLK), BF16),
        pltpu.VMEM((4, BLK, K), BF16),
        pltpu.VMEM((ROWS, 2 * BLK), BF16),
        pltpu.VMEM((BLK, K), BF16),
        pltpu.VMEM((ROWS, K), F32),
        pltpu.VMEM((4, BLK, K), BF16),
        pltpu.VMEM((4, BLK, K), BF16),
        pltpu.VMEM((2, BLK, K), BF16),
        pltpu.VMEM((K, BLK), BF16),
        pltpu.VMEM((K, BLK), F32),
        pltpu.VMEM((K, BLK), BF16),
        pltpu.VMEM((K, BLK), BF16),
        pltpu.VMEM((2, 2 * SCEN_L, BLK), F32),
        pltpu.VMEM((2, 2 * SCEN_L, BLK), F32),
        pltpu.VMEM((2, 2 * SCEN_L, BLK), F32),
        pltpu.VMEM((NZ, TILE, BLK), F32),
        pltpu.VMEM((nz, TILE, BLK), F32),
        pltpu.VMEM((TILE, BLK), F32),
        pltpu.VMEM((nx, TILE, BLK), F32),
        pltpu.VMEM((CHUNK, K), F32),
        pltpu.VMEM((NZ, CHUNK, K), F32),
        pltpu.VMEM((4, NX, 8, BLK), F32),
        pltpu.VMEM((BLK + 16, BLK), F32),
        pltpu.VMEM((BLK + 16, BLK), F32),
        pltpu.VMEM((BLK + 16, BLK), F32),
        dma((4,)), dma((2, 2)), dma((2, 2)), dma, dma, dma, dma, dma, dma((nz,)),
        dma, dma, dma((2,)), dma((2,)),
    ]

    def padded(rows, top):
        return jnp.pad(rows, ((top, 16 - top - rows.shape[0]), (0, BLK - rows.shape[1])))

    small = padded(node_of, 0) + padded(line_class, 9) + padded(res_count.reshape(1, 1), 10)
    small = small.astype(F32) + padded(tie_coef, 8)
    node_mean, base, live = pl.pallas_call(
        kernel,
        out_shape=[jax.ShapeDtypeStruct(flat, F32)] * 2 + [jax.ShapeDtypeStruct((8, BLK), F32)],
        in_specs=[hbm] * 4 + [vmem],
        out_specs=[vmem] * 3,
        scratch_shapes=scratch,
        compiler_params=pltpu.CompilerParams(
            collective_id=0, has_side_effects=True, vmem_limit_bytes=105 * 2**19
        ),
        name="round",
    )(
        cost_lin.reshape(flat), na_dual.reshape(flat), prior_mean.reshape(flat),
        kkt_inverse.reshape(SPANS, K, K), small,
    )
    node_mean = node_mean * live[0:1]
    new_dual = base - node_mean
    return node_mean.reshape(cost_lin.shape), new_dual.reshape(cost_lin.shape)


def solution(mesh):
    placed = (
        P("scen", "area", None, None),
        P("scen", "area", None, None),
        P("scen", "area", None, None),
        P("area", None, None, None),
        P("area", None),
        P("area"),
        P("area", None),
        P(None, "scen"),
    )
    return jax.shard_map(
        on_device,
        mesh=mesh,
        in_specs=placed,
        out_specs=(P("scen", "area", None, None), P("scen", "area", None, None)),
        check_vma=False,
    )
```
